32 devices in a mesh: head: 4 (over y, x), expert: 8 (over z, core).
Axes of the slice: x: 2, y: 2, z: 4, core: 2. Of those that a mesh axis runs over, the one named last changes fastest.
Arguments:
- block_entries: bfloat16 [16, 1024, 768], P('expert', 'head'), may hold values from -6 to 6
- passage_labels: int32 [16, 1024], P('expert'), may hold values from 0 to 4, as said below
- assigned_specialist: int32 [16, 1024], P('expert', 'head'), may hold values from 0 to 7, as said below
- buffer_places: int32 [16, 1024], P('expert', 'head'), may hold values from -1 to 63, as said below
- mixing_scaling_factor: float32 [768], replicated, may hold values from 0.25 to 1.75
- asker_projection: bfloat16 [768, 768], P(None, 'head'), may hold values from -0.3125 to 0.3125
- address_projection: bfloat16 [768, 768], P(None, 'head'), may hold values from -0.3125 to 0.3125
- content_projection: bfloat16 [768, 768], P(None, 'head'), may hold values from -0.21875 to 0.21875
- final_mixing_projection: bfloat16 [768, 768], P('head'), may hold values from -0.875 to 0.875
- specialist_scaling_factor: float32 [768], replicated, may hold values from 0.25 to 1.75
- dispatcher_projection: float32 [768, 16], replicated, may hold values from -0.21875 to 0.21875
- specialist_anchors_vector: float32 [8, 16], replicated, may hold values from -6 to 6
- softening_coefficient: float32 [1], replicated, may hold values from 0.25 to 0.45
- specialist_widen_factors: bfloat16 [8, 768, 3072], P('expert', None, 'head'), may hold values from -0.21875 to 0.21875
- specialist_shrink_factors: bfloat16 [8, 3072, 768], P('expert', 'head'), may hold values from -1 to 1
- incoming_gradient: bfloat16 [16, 1024, 768], P('expert', 'head'), may hold values from -6 to 6
Outputs:
- output: bfloat16 [16, 1024, 768], P('expert', 'head')
- grad_tokens: float32 [16, 1024, 768], P('expert', 'head')
- grad_gain_attn: float32 [768], replicated
- grad_query: float32 [768, 768], P(None, 'head')
- grad_key: float32 [768, 768], P(None, 'head')
- grad_value: float32 [768, 768], P(None, 'head')
- grad_output: float32 [768, 768], P('head')
- grad_gain_moe: float32 [768], replicated
- grad_router: float32 [768, 16], replicated
- grad_embed: float32 [8, 16], replicated
- grad_temperature: float32 [1], replicated
- grad_in: float32 [8, 768, 3072], P('expert', None, 'head')
- grad_out: float32 [8, 3072, 768], P('expert', 'head')
- load: float32 [8], replicated
The draws below stay inside these ranges and needn't reach their ends.
Inputs may be any that keep to these rules, and one draw needn't show every extreme that they name: `passage_labels`: each sequence holds documents numbered from 0 upward in order of position, never falling, all of 0 to 4 present. `assigned_specialist`: the expert that each token is sent to. `buffer_places`: over the rows of one device, taken in the order of sequence then position, a token's rank among that device's tokens with the same route, or -1 where that rank is 64 or more.
All inputs are finite; a program needn't handle non-finite values.
Results may differ from the reference program's by a relative error of at most 0.014.
The reference program's roundings to bfloat16 on the way count: a program that leaves them out, or rounds other values in their place, can miss the bound.
Values may be sent and summed in bfloat16 or wider, within the bound.
No kernel may reach another device: no remote copies, remote signals or barrier semaphores. Data moves between devices by JAX's collectives and lax.ppermute only.
A program may use at most 128 MiB of HBM per device.

```python
import math
import jax
import jax.numpy as jnp
from jax import lax

D = 768
HEADS = 12
HSZ = 64
FF = 3072
RDIM = 16
SEQ = 1024
SEQS = 2
EXPERTS = 8
HD = 768
CAP = 64
SEQS_ALL = 16
TOKENS = 16384
N_HEAD = 4
N_EXPERT = 8


def route_blocks(key):
    row_count = SEQS * SEQ // N_HEAD
    capacity = row_count // EXPERTS
    block_count = N_EXPERT * N_HEAD
    key_base, key_hot, key_order = jax.random.split(key, 3)
    random_base = jax.random.randint(key_base, (block_count, row_count), 0, EXPERTS)
    hot_expert = jax.random.randint(key_hot, (block_count, 1), 0, EXPERTS)
    order_keys = jax.random.split(key_order, block_count)

    def shuffled(subkey):
        return jax.random.permutation(subkey, row_count)
    ranking = jax.vmap(shuffled)(order_keys)
    chosen = jnp.where(ranking < 2 * capacity, hot_expert, random_base).astype(jnp.int32)
    onehot = (chosen[:, :, None] == jnp.arange(EXPERTS)[None, None, :]).astype(jnp.int32)
    earlier = jnp.cumsum(onehot, axis=1) - onehot
    position = jnp.sum(earlier * onehot, axis=2)
    position = jnp.where(position < capacity, position, -1).astype(jnp.int32)

    def arrange(values):
        return values.reshape(N_EXPERT, N_HEAD, SEQS, SEQ // N_HEAD).transpose(0, 2, 1, 3).reshape(N_EXPERT * SEQS, SEQ)
    return (arrange(chosen), arrange(position))


def draw_assigned_specialist(key, part):
    chosen, position = route_blocks(key)
    return chosen


def draw_buffer_places(key, part):
    chosen, position = route_blocks(key)
    return position


def draw_passage_labels(key, part):
    key = jax.random.fold_in(key, 7)
    key_one, key_two, key_three, key_four = jax.random.split(key, 4)
    seq_total = SEQS * N_EXPERT
    eighth = SEQ // 8
    first_cut = jax.random.randint(key_one, (seq_total, 1), 1, eighth)
    second_cut = first_cut + jax.random.randint(key_two, (seq_total, 1), 1, eighth)
    third_cut = SEQ - SEQ // 4 + jax.random.randint(key_three, (seq_total, 1), 0, eighth)
    fourth_cut = third_cut + jax.random.randint(key_four, (seq_total, 1), 1, eighth)
    places = jnp.arange(SEQ)[None, :]
    doc_ids = (places >= first_cut).astype(jnp.int32) + (places >= second_cut).astype(jnp.int32)
    doc_ids = doc_ids + (places >= third_cut).astype(jnp.int32) + (places >= fourth_cut).astype(jnp.int32)
    return doc_ids.astype(jnp.int32)


def block_levels(own_key, shape, pieces, smallest, high):
    loudness = 1.0
    for dim, parts in pieces:
        steps = jax.random.uniform(jax.random.fold_in(jax.random.fold_in(own_key, 6), dim), (parts,), jnp.float32, smallest / len(pieces), high / len(pieces))
        loudness = loudness * jnp.repeat(jnp.exp(steps), shape[dim] // parts).reshape((-1,) + (1,) * (len(shape) - 1 - dim))
    return loudness


def scatter_about(stream_key, dims, scale, reach, pieces=(), held_as=jnp.bfloat16):
    values = scale * jax.random.normal(stream_key, dims, jnp.float32)
    if pieces:
        values = values * block_levels(stream_key, dims, pieces, -0.22, 0.18)
    return jnp.clip(values, -reach, reach).astype(held_as)


def setup_inputs(seed: int = 0) -> dict:
    keys = jax.random.split(jax.random.key(seed), 17)
    block_entries = scatter_about(keys[0], (SEQS_ALL, SEQ, D), 1.0, 6.0, ((0, 8), (1, 4)))
    passage_labels = draw_passage_labels(jax.random.fold_in(keys[16], 71), 0)
    assigned_specialist = draw_assigned_specialist(jax.random.fold_in(keys[16], 71), 0)
    buffer_places = draw_buffer_places(jax.random.fold_in(keys[16], 71), 0)
    mixing_scaling_factor = jnp.clip(1.0 + 0.15 * jax.random.normal(keys[4], (D,), jnp.float32), 0.25, 1.75)
    asker_projection = scatter_about(keys[5], (D, HD), (D // 2) ** -0.5, 0.3125, ((1, 4),))
    address_projection = scatter_about(keys[6], (D, HD), (D // 2) ** -0.5, 0.3125, ((1, 4),))
    content_projection = scatter_about(keys[7], (D, HD), D ** -0.5, 0.21875, ((1, 4),))
    final_mixing_projection = scatter_about(keys[8], (HD, D), (HD // 16) ** -0.5, 0.875, ((0, 4),))
    specialist_scaling_factor = jnp.clip(1.0 + 0.15 * jax.random.normal(keys[9], (D,), jnp.float32), 0.25, 1.75)
    dispatcher_projection = scatter_about(keys[10], (D, RDIM), D ** -0.5, 0.21875, (), jnp.float32)
    specialist_anchors_vector = scatter_about(keys[11], (EXPERTS, RDIM), 1.0, 6.0, (), jnp.float32)
    softening_coefficient = jnp.clip(jnp.exp(jax.random.uniform(keys[12], (1,), jnp.float32, math.log(0.25), math.log(0.45))), 0.25, 0.45)
    specialist_widen_factors = scatter_about(keys[13], (EXPERTS, D, FF), D ** -0.5, 0.21875, ((0, 8), (2, 4)))
    specialist_shrink_factors = scatter_about(keys[14], (EXPERTS, FF, D), (0.02 * EXPERTS), 1.0, ((0, 8), (1, 4)))
    incoming_gradient = scatter_about(keys[15], (SEQS_ALL, SEQ, D), 1.0, 6.0, ((0, 8), (1, 4)))
    return {"block_entries": block_entries, "passage_labels": passage_labels, "assigned_specialist": assigned_specialist, "buffer_places": buffer_places, "mixing_scaling_factor": mixing_scaling_factor, "asker_projection": asker_projection, "address_projection": address_projection, "content_projection": content_projection, "final_mixing_projection": final_mixing_projection, "specialist_scaling_factor": specialist_scaling_factor, "dispatcher_projection": dispatcher_projection, "specialist_anchors_vector": specialist_anchors_vector, "softening_coefficient": softening_coefficient, "specialist_widen_factors": specialist_widen_factors, "specialist_shrink_factors": specialist_shrink_factors, "incoming_gradient": incoming_gradient}


HIGHEST = lax.Precision.HIGHEST
NEG_FILL = -1e+30

@jax.custom_vjp
def low(v):
    return lax.optimization_barrier(v.astype(jnp.bfloat16)).astype(jnp.float32)

@jax.custom_vjp
def low_back(v):
    return v

def low_keep(v):
    return (low(v), None)

def low_pass(kept, grad):
    return (grad,)

def back_keep(v):
    return (v, None)

def back_low(kept, grad):
    return (low(grad),)
low.defvjp(low_keep, low_pass)
low_back.defvjp(back_keep, back_low)

def layer_norm(values, gain_vec):
    center = values - lax.optimization_barrier(jnp.mean(values, axis=-1, keepdims=True))
    spread = lax.optimization_barrier(jnp.mean(center * center, axis=-1, keepdims=True))
    return center * lax.rsqrt(spread + 1e-05) * gain_vec

def attend_sequence(packed):
    query_rows, key_rows, value_rows, segment = packed
    score_scale = HSZ ** (-0.5)
    scores = low_back(jnp.einsum('qhd,khd->hqk', query_rows, key_rows, precision=HIGHEST) * score_scale)
    allowed = segment[:, None] == segment[None, :]
    scores = jnp.where(allowed[None], scores, NEG_FILL)
    prob_rows = low(jax.nn.softmax(scores, axis=-1))
    return jnp.einsum('hqk,khd->qhd', prob_rows, value_rows, precision=HIGHEST)

def expert_block(packed):
    inputs, first_w, second_w = packed
    pre_act = low_back(jnp.dot(inputs, first_w, precision=HIGHEST))
    hidden = low(jax.nn.gelu(pre_act))
    return jnp.dot(hidden, second_w, precision=HIGHEST)

def router_gate(flat_rows, weight, embed_rows, temper, chosen):
    projected = jnp.dot(flat_rows, weight, precision=HIGHEST)
    unit_rows = projected * lax.rsqrt(lax.optimization_barrier(jnp.sum(projected * projected, axis=-1, keepdims=True)) + 1e-06)
    anchor = embed_rows * lax.rsqrt(lax.optimization_barrier(jnp.sum(embed_rows * embed_rows, axis=-1, keepdims=True)) + 1e-06)
    logits = jnp.dot(unit_rows, anchor.T, precision=HIGHEST) / temper[0]
    prob_rows = jax.nn.softmax(logits, axis=-1)
    return lax.optimization_barrier(jnp.sum(prob_rows * chosen, axis=-1))

def reference(block_entries, passage_labels, assigned_specialist, buffer_places, mixing_scaling_factor, asker_projection, address_projection, content_projection, final_mixing_projection, specialist_scaling_factor, dispatcher_projection, specialist_anchors_vector, softening_coefficient, specialist_widen_factors, specialist_shrink_factors, incoming_gradient):
    route_flat = assigned_specialist.reshape(TOKENS)
    chosen = (route_flat[:, None] == jnp.arange(EXPERTS).astype(jnp.int32)[None, :]).astype(jnp.float32)
    slot_count = N_EXPERT * N_HEAD * CAP
    seq_index = jnp.arange(SEQS_ALL).astype(jnp.int32)
    pos_index = jnp.arange(SEQ).astype(jnp.int32)
    source = seq_index[:, None] // SEQS * N_HEAD + pos_index[None, :] // (SEQ // N_HEAD)
    kept_mask = (buffer_places >= 0).reshape(TOKENS)
    row_index = (assigned_specialist * slot_count + source * CAP + jnp.maximum(buffer_places, 0)).reshape(TOKENS).astype(jnp.int32)

    def forward(tok_f, gain_a, query_w, key_w, value_w, out_w, gain_m, router_w, embed_w, temper, first_w, second_w):
        normed = low(layer_norm(tok_f, gain_a))

        def project(weight):
            return low_back(low(jnp.dot(normed, weight, precision=HIGHEST))).reshape(SEQS_ALL, SEQ, HEADS, HSZ)
        attended = lax.map(jax.checkpoint(attend_sequence), (project(query_w), project(key_w), project(value_w), passage_labels))
        mixed_rows = low_back(low(attended.reshape(SEQS_ALL, SEQ, HD)))
        branch = low_back(jnp.dot(mixed_rows, out_w, precision=HIGHEST))
        middle = tok_f + branch
        normed_moe = low(layer_norm(middle, gain_m))
        flat_rows = normed_moe.reshape(TOKENS, D)
        gating = router_gate(flat_rows, router_w, embed_w, temper, chosen)
        sent_rows = low_back(flat_rows)
        buffer = jnp.zeros((EXPERTS * slot_count, D), jnp.float32).at[row_index].add(jnp.where(kept_mask[:, None], sent_rows, 0.0))
        expert_rows = lax.map(jax.checkpoint(expert_block), (buffer.reshape(EXPERTS, slot_count, D), first_w, second_w))
        returned = low_back(low(expert_rows)).reshape(EXPERTS * slot_count, D)
        token_out = jnp.where(kept_mask[:, None], returned[row_index], 0.0)
        result = middle.reshape(TOKENS, D) + gating[:, None] * token_out
        return result.reshape(SEQS_ALL, SEQ, D)
    real_valued_operands = (block_entries.astype(jnp.float32), mixing_scaling_factor.astype(jnp.float32), asker_projection.astype(jnp.float32), address_projection.astype(jnp.float32), content_projection.astype(jnp.float32), final_mixing_projection.astype(jnp.float32), specialist_scaling_factor.astype(jnp.float32), dispatcher_projection.astype(jnp.float32), specialist_anchors_vector.astype(jnp.float32), softening_coefficient.astype(jnp.float32), specialist_widen_factors.astype(jnp.float32), specialist_shrink_factors.astype(jnp.float32))
    output, pullback = jax.vjp(forward, *real_valued_operands)
    gradients = pullback(incoming_gradient.astype(jnp.float32))
    load_share = lax.optimization_barrier(jnp.sum(chosen, axis=0)) * EXPERTS / TOKENS
    return (output.astype(jnp.bfloat16), gradients[0], gradients[1], gradients[2], gradients[3], gradients[4], gradients[5], gradients[6], gradients[7], gradients[8], gradients[9], gradients[10], gradients[11], load_share)
```

```python
import functools

import jax
import jax.numpy as jnp
from jax import lax
from jax.experimental import pallas as pl
from jax.experimental.pallas import tpu as pltpu
from jax.sharding import PartitionSpec as P

HSZ = 64
F32 = jnp.float32
BF16 = jnp.bfloat16
HIGHEST = lax.Precision.HIGHEST
NEG_FILL = -1e30
MIB = 2**20
EXTRA = 16
CHUNK = 256
BESIDE = 2.0
ATTEND = 11.0
ATTEND_BACK = 15.0
BACK_FIRST = 15.0
FINAL = 2.0
SUMS = 5.0

NN = ((1,), (0,))
NT = ((1,), (1,))
TN = ((0,), (0,))


def dot(lhs, rhs, dims=NN, precision=None):
    return lax.dot_general(
        lhs, rhs, (dims, ((), ())), precision=precision, preferred_element_type=F32
    )


def call(body, outs, args, scratch=(), limit=14, micros=0.02, smem=0, kept=0):
    name = (body.func if isinstance(body, functools.partial) else body).__name__
    spaces = [out[2] if len(out) > 2 else pltpu.VMEM for out in outs]
    return pl.pallas_call(
        body,
        out_shape=[
            pltpu.HBM(out[0], out[1])
            if space == pltpu.HBM
            else jax.ShapeDtypeStruct(out[0], out[1])
            for out, space in zip(outs, spaces)
        ],
        in_specs=[pl.BlockSpec(memory_space=pltpu.SMEM)] * smem
        + [pl.BlockSpec(memory_space=pltpu.VMEM)] * (len(args) - smem - kept)
        + [pl.BlockSpec(memory_space=pltpu.HBM)] * kept,
        out_specs=[pl.BlockSpec(memory_space=space) for space in spaces],
        scratch_shapes=list(scratch),
        compiler_params=pltpu.CompilerParams(vmem_limit_bytes=limit * MIB),
        cost_estimate=pl.CostEstimate(
            flops=int(micros * 1.15e9), bytes_accessed=0, transcendentals=0
        ),
        name=name,
    )(
        *args[: len(args) - kept],
        *(pltpu.with_memory_space_constraint(v, pltpu.HBM) for v in args[len(args) - kept :]),
    )


class Order:
    def __init__(self):
        self.last = ()

    def __call__(self, values):
        return lax.optimization_barrier((values, self.last))[0]

    def mark(self, *values):
        self.last = values

    def arrived(self, *values):
        self.last = (*self.last, *values)


def split3(values):
    high = values.astype(BF16)
    rest = values - high.astype(F32)
    mid = rest.astype(BF16)
    low = (rest - mid.astype(F32)).astype(BF16)
    return high, mid, low


def normalize(values):
    center = values - jnp.mean(values, axis=-1, keepdims=True)
    scale = lax.rsqrt(jnp.mean(center * center, axis=-1, keepdims=True) + 1e-05)
    return center * scale, scale


def normalize_back(unit, scale, grad):
    return scale * (
        grad
        - jnp.mean(grad, axis=-1, keepdims=True)
        - unit * jnp.mean(grad * unit, axis=-1, keepdims=True)
    )


def norm_kernel(s, x_ref, gain_ref, *outs):
    chunk = 64
    count = outs[0].shape[0]
    for part, out_ref in enumerate(outs):
        start = (s + part) * count

        def body(i, carry, out_ref=out_ref, start=start):
            rows = pl.ds(pl.multiple_of(start + i * chunk, chunk), chunk)
            unit, _ = normalize(x_ref[rows, :].astype(F32))
            out_ref[pl.ds(pl.multiple_of(i * chunk, chunk), chunk), :] = (
                unit * gain_ref[...]
            ).astype(BF16)
            return carry

        lax.fori_loop(0, count // chunk, body, 0)


def prep_kernel(experts, head_ref, expert_ref, labels_ref, route_ref, slot_ref, *outs):
    *label_outs, route_out, send_out, back_out = outs
    seqs, length = labels_ref.shape
    span = route_ref.shape[1]
    for s, out in enumerate(label_outs):
        for k in range(length // span):
            at = pl.ds(pl.multiple_of((head_ref[0] ^ k) * span, span), span)
            out[:, k * span : (k + 1) * span] = labels_ref[s : s + 1, at]
    route = jnp.concatenate([route_ref[s : s + 1, :] for s in range(seqs)], axis=1)
    slot = jnp.concatenate([slot_ref[s : s + 1, :] for s in range(seqs)], axis=1)
    rows = seqs * span
    capacity = rows // experts
    to = route ^ jnp.full(route.shape, expert_ref[0], jnp.int32)
    side, place = to & 1, to >> 1
    route_out[...] = route
    send_out[...] = jnp.where(slot >= 0, (side * (experts // 2) + place) * capacity + slot, -1)
    back = place * capacity + slot + jnp.where(side == 0, place * capacity, rows)
    back_out[...] = as_column(jnp.where(slot >= 0, back, -1)).astype(jnp.int32)


def head_mask(rows, width, head):
    lane = lax.broadcasted_iota(jnp.int32, (rows, width), 1)
    return (lane // HSZ) == head


def as_column(row):
    return jnp.broadcast_to(row.astype(F32), (8, row.shape[1])).T[:, 0:1]


def attend_kernel(earlier, *refs):
    count = len(refs) - 22 - earlier
    blocks = refs[:count]
    before = refs[count : count + earlier]
    count += earlier
    (wq, wk, wv, seg_row, q_out, k_out, v_out, all_out, out_out, m0, m1, m2, m3, lse_ref,
     q_ref, k_ref, v_ref, kh_ref, vt_ref, mix_ref, seg_col, sems) = refs[count:]
    length, width = q_ref.shape
    heads = width // HSZ
    scale = HSZ ** (-0.5)
    seg_col[...] = as_column(seg_row[...])
    off = 0
    copies = []
    for i, ref in enumerate(blocks):
        rows = ref.shape[0]
        at = slice(off, off + rows)
        copies.append(pltpu.make_async_copy(ref, all_out.at[pl.ds(off, rows)], sems.at[4 + i]))
        copies[-1].start()
        block = ref[...]
        queries = dot(block, wq[...], NT).astype(BF16)
        q_ref[at, :] = (queries.astype(F32) * scale).astype(BF16)
        keys = dot(block, wk[...], NT).astype(BF16)
        k_ref[at, :] = keys
        keys = keys.astype(F32)
        for j in range(heads):
            kh_ref[j, at, :] = jnp.where(head_mask(rows, width, j), keys, 0.0).astype(BF16)
        v_ref[at, :] = dot(block, wv[...], NT).astype(BF16)
        vt_ref[:, at] = dot(wv[...], block, NT).astype(BF16)
        off += rows
    for i, (ref, out) in enumerate(((q_ref, q_out), (k_ref, k_out), (v_ref, v_out))):
        copies.append(pltpu.make_async_copy(ref, out, sems.at[i]))
        copies[-1].start()
    block_len = length // 4

    def body(b, carry):
        at = pl.ds(pl.multiple_of(b * block_len, block_len), block_len)
        queries = q_ref[at, :]
        allowed = seg_col[...] == seg_row[:, at].astype(F32)
        outs = []
        for j in range(heads):
            scores = jnp.where(allowed, dot(kh_ref[j], queries, NT), NEG_FILL)
            peak = jnp.max(scores, axis=0, keepdims=True)
            probs = jnp.exp(scores - peak)
            total = jnp.sum(probs, axis=0, keepdims=True)
            outs.append(dot(vt_ref[j * HSZ : (j + 1) * HSZ, :], probs.astype(BF16)) / total)
            lse_ref[j : j + 1, at] = peak + jnp.log(total)
        mix_ref[:, at] = jnp.concatenate(outs, axis=0)
        return carry

    lax.fori_loop(0, 4, body, 0, unroll=4)
    copies.append(pltpu.make_async_copy(mix_ref, out_out, sems.at[3]))
    copies[-1].start()
    for i, ref in enumerate((m0, m1, m2, m3)):
        start = ref.shape[1] - block_len
        if before:
            ref[:, 0:start] = before[i][...]
        ref[:, start:] = mix_ref[:, i * block_len : (i + 1) * block_len].astype(BF16)
    for copy in copies:
        copy.wait()


def attend_back_kernel(
    s, q_ref, k_ref, v_ref, out_ref, g0, g1, g2, g3, lse_ref, seg_row, wq_kept, wk_kept, wv_kept,
    dq_ref, dk_ref, dv_ref, own_ref, keep_a, keep_b, to_x, to_y,
    kh_ref, vh_ref, kt_ref, g_ref, dk_acc, dv_acc, seg_col, prob_ref, grad_ref, wq, wk, wv, sems,
):
    copies = [
        pltpu.make_async_copy(kept, ref, sems.at[i])
        for i, (kept, ref) in enumerate(((wq_kept, wq), (wk_kept, wk), (wv_kept, wv)))
    ]
    for copy in copies:
        copy.start()
    length, width = q_ref.shape
    heads = width // HSZ
    scale = HSZ ** (-0.5)
    block_len = length // 4
    for i, ref in enumerate((g0, g1, g2, g3)):
        at = slice(i * block_len, (i + 1) * block_len)
        g_ref[:, at] = ref[:, s * block_len : (s + 1) * block_len]
        keys = k_ref[at, :].astype(F32)
        kt_ref[:, at] = keys.T.astype(BF16)
        values = v_ref[at, :].astype(F32)
        for j in range(heads):
            mask = head_mask(block_len, width, j)
            kh_ref[j, at, :] = jnp.where(mask, keys, 0.0).astype(BF16)
            vh_ref[j, at, :] = jnp.where(mask, values, 0.0).astype(BF16)
    seg_col[...] = as_column(seg_row[...])
    dk_acc[...] = jnp.zeros_like(dk_acc)
    dv_acc[...] = jnp.zeros_like(dv_acc)

    def body(b, carry):
        at = pl.ds(pl.multiple_of(b * block_len, block_len), block_len)
        queries = q_ref[at, :]
        grads = g_ref[:, at]
        row = seg_row[:, at].astype(F32)
        masks = [head_mask(block_len, width, j) for j in range(heads)]

        def per_head(values):
            values = values.astype(F32)
            return jnp.concatenate(
                [jnp.where(mask, values, 0.0).astype(BF16) for mask in masks], axis=0
            )

        def head_rows(values, j):
            rest = [(j * HSZ, 0), (width - (j + 1) * HSZ, 1)]
            zeros = [jnp.zeros((rows, block_len), BF16) for rows, _ in rest]
            own = values[j * HSZ : (j + 1) * HSZ, :]
            parts = [zeros[0], own, zeros[1]]
            return jnp.concatenate([part for part in parts if part.shape[0]], axis=0)

        dqs = []
        weighted = grads.astype(F32) * out_ref[:, at]
        for j in range(heads):
            at_head = slice(j * HSZ, (j + 1) * HSZ)
            lanes = slice(j * block_len, (j + 1) * block_len)
            delta = jnp.sum(weighted[at_head, :], axis=0, keepdims=True)
            lse = lse_ref[j : j + 1, at]
            for c in range(0, length, CHUNK):
                keys = slice(c, c + CHUNK)
                scores = dot(kh_ref[j, keys, :], queries, NT)
                probs = jnp.where(seg_col[keys, :] == row, jnp.exp(scores - lse), 0.0)
                prob_ref[keys, lanes] = probs.astype(BF16)
                grad = probs * (dot(vh_ref[j, keys, :], grads) - delta)
                grad_ref[keys, lanes] = grad.astype(BF16)
            dqs.append(dot(kt_ref[at_head, :], grad_ref[:, lanes]))
        dv_acc[...] += dot(
            prob_ref[...],
            jnp.concatenate([head_rows(grads, j) for j in range(heads)], axis=1),
            NT,
        )
        dk_acc[...] += dot(grad_ref[...], per_head(queries))
        dq = (jnp.concatenate(dqs, axis=0) * scale).T
        dq_ref[at, :] = dq.astype(BF16)
        return carry

    lax.fori_loop(0, 4, body, 0)
    dk_ref[...] = dk_acc[...].astype(BF16)
    dv_ref[...] = dv_acc[...].astype(BF16)
    for copy in copies:
        copy.wait()
    half = block_len // 2
    for i in range(8):
        at = slice(i * half, (i + 1) * half)
        rows = (
            dot(dq_ref[at, :], wq[...])
            + dot(dk_ref[at, :], wk[...])
            + dot(dv_ref[at, :], wv[...])
        )
        block, part = i // 2, i % 2
        if block == 0:
            own_ref[at, :] = rows
        elif block == 1 and part == 0:
            to_x[0:half, :] = rows.astype(BF16)
        elif block == 1:
            keep_b[...] = rows
        elif block == 2 and part == 0:
            keep_a[...] = rows
        elif block == 2:
            to_y[0:half, :] = rows.astype(BF16)
        elif part == 0:
            to_x[half:, :] = rows.astype(BF16)
        else:
            to_y[half:, :] = rows.astype(BF16)


def route_forward(normed, split_router, embed, temper, route_row):
    depth = embed.shape[1]
    parts = dot(split_router, normed, NT)
    projected = parts[0:depth] + parts[depth : 2 * depth] + parts[2 * depth : 3 * depth]
    length = lax.rsqrt(jnp.sum(projected * projected, axis=0, keepdims=True) + 1e-06)
    unit = projected * length
    anchor = embed * lax.rsqrt(jnp.sum(embed * embed, axis=1, keepdims=True) + 1e-06)
    logits = dot(anchor, unit, precision=HIGHEST) / temper
    powers = jnp.exp(logits - jnp.max(logits, axis=0, keepdims=True))
    probs = powers / jnp.sum(powers, axis=0, keepdims=True)
    chosen = (lax.broadcasted_iota(jnp.int32, probs.shape, 0) == route_row).astype(F32)
    gating = jnp.sum(probs * chosen, axis=0, keepdims=True)
    return projected, length, unit, logits, probs, chosen, gating


def middle_kernel(*refs):
    (m0, m1, m2, m3, w0, far_ref, x_ref, gain_ref,
     router_ref, embed_ref, temper_ref, route_ref, col_ref, g_ref,
     middle_out, normed_out, mixed_out, far_out, grad_out_a, grad_out_b, ta, tb,
     middle_ref, normed_ref, ga, gb, sems) = refs
    chunk = 128
    width = m0.shape[0]
    stash = [pltpu.make_async_copy(far_ref, far_out, sems.at[4])]
    for k, ref in enumerate((m0, m1, m2, m3)):
        out = mixed_out.at[pl.ds(k * width, width)]
        stash.append(pltpu.make_async_copy(ref, out, sems.at[5 + k]))
    for copy in stash:
        copy.start()
    for i in range(x_ref.shape[0] // chunk):
        at = slice(i * chunk, (i + 1) * chunk)
        rows = dot(m0[:, at], w0[...], TN)
        for k, ref in enumerate((m1, m2, m3)):
            rows += dot(ref[:, at], far_ref[k * width : (k + 1) * width, :], TN)
        rows += x_ref[at, :].astype(F32)
        middle_ref[at, :] = rows
        unit, _ = normalize(rows)
        normed_ref[at, :] = (unit * gain_ref[...]).astype(BF16)
    copies = [
        pltpu.make_async_copy(middle_ref, middle_out, sems.at[0]),
        pltpu.make_async_copy(normed_ref, normed_out, sems.at[1]),
    ]
    for copy in copies:
        copy.start()
    normed = normed_ref[...]
    gating = route_forward(
        normed, router_ref[...], embed_ref[...], temper_ref[...], route_ref[...]
    )[-1]
    count = normed.shape[0]
    slots = ta.shape[0]
    last = (grad_out_a, grad_out_b)
    for part, (tok_out, grad_out) in enumerate(((ta, ga), (tb, gb))):
        slot = lax.broadcasted_iota(jnp.int32, (slots, count), 0) + part * slots
        match = slot == col_ref[...]
        place = jnp.where(match, 1.0, 0.0).astype(BF16)
        tok_out[...] = dot(place, normed).astype(BF16)
        amount = jnp.sum(jnp.where(match, gating, 0.0), axis=1, keepdims=True)
        grad_out[...] = (dot(place, g_ref[...]) * amount).astype(BF16)
        copies.append(pltpu.make_async_copy(grad_out, last[part], sems.at[2 + part]))
        copies[-1].start()
    for copy in stash + copies:
        copy.wait()


def cores_kernel(first, near, *outs):
    size = outs[0].shape[0] // 2
    for k, out in enumerate(outs):
        at = slice(k * size, (k + 1) * size)
        out[0:size, :] = first[at, :]
        out[size:, :] = near[at, :]


def half_kernel(*refs):
    gather_pieces(refs[:-1], refs[-1])


def second_kernel(count, *refs):
    pieces, rest, out_ref = refs[:count], refs[count:-1], refs[-1]
    size = pieces[0].shape[0] // 2
    for k, ref in enumerate(pieces):
        out_ref[k * size : (k + 1) * size, :] = ref[size:, :]
    for ref in rest:
        out_ref[count * size :, :] = ref[...]


def gelu_both(pre):
    root = 0.7978845608028654
    cube = 0.044715
    square = pre * pre
    wave = jnp.tanh(root * pre * (1.0 + cube * square))
    half = 0.5 * (1.0 + wave)
    slope = half + 0.5 * pre * (1.0 - wave * wave) * (root * (1.0 + 3.0 * cube * square))
    return pre * half, slope


def gather_pieces(pieces, out_ref):
    start = 0
    for ref in pieces:
        out_ref[start : start + ref.shape[0], :] = ref[...]
        start += ref.shape[0]


def scatter_pieces(start, rows, pieces):
    size = pieces[0].shape[0]
    for k, ref in enumerate(pieces):
        if start <= k * size < start + rows.shape[0]:
            ref[...] = rows[k * size - start : (k + 1) * size - start, :].astype(ref.dtype)


def stash_rows(ref, out_ref, at, sem):
    rows = pl.ds(at.start, at.stop - at.start)
    copy = pltpu.make_async_copy(ref.at[rows], out_ref.at[rows], sem)
    copy.start()
    return copy


def expert_kernel(count, *refs):
    pieces = refs[:count]
    in0, out0, far, x_out, h_out, x_ref, h1, p0, p1 = refs[count : count + 9]
    *outs, h0, sems = refs[count + 9 :]
    model = in0.shape[0]
    gather_pieces(pieces, x_ref)
    copies = [stash_rows(x_ref, x_out, slice(0, x_ref.shape[0]), sems.at[0])]
    chunk = 256
    for i in range(x_ref.shape[0] // chunk):
        at = slice(i * chunk, (i + 1) * chunk)
        rows = x_ref[at, :]
        total = None
        for first, second, h_ref, p_ref in (
            (in0, out0, h0, p0),
            (far.at[0:model], far.at[model:], h1, p1),
        ):
            hidden, slope = gelu_both(dot(rows, first[...]))
            hidden = hidden.astype(BF16)
            h_ref[at, :] = hidden
            p_ref[at, :] = slope
            part = dot(hidden, second[...])
            total = part if total is None else total + part
        copies.append(stash_rows(h0, h_out, at, sems.at[1 + i]))
        scatter_pieces(i * chunk, total, outs)
    for copy in copies:
        copy.wait()


def expert_back_kernel(count, *refs):
    pieces = refs[:count]
    in0, out0, far, p0, p1, dy_out, d_out, dy_ref, d1 = refs[count : count + 9]
    *outs, d0, sems = refs[count + 9 :]
    model = in0.shape[0]
    gather_pieces(pieces, dy_ref)
    copies = [stash_rows(dy_ref, dy_out, slice(0, dy_ref.shape[0]), sems.at[0])]
    chunk = 256
    for i in range(dy_ref.shape[0] // chunk):
        at = slice(i * chunk, (i + 1) * chunk)
        rows = dy_ref[at, :]
        total = None
        for first, second, p_ref, d_ref in (
            (in0, out0, p0, d0),
            (far.at[0:model], far.at[model:], p1, d1),
        ):
            grad = (dot(rows, second[...], NT) * p_ref[at, :]).astype(BF16)
            d_ref[at, :] = grad
            part = dot(grad, first[...], NT)
            total = part if total is None else total + part
        copies.append(stash_rows(d0, d_out, at, sems.at[1 + i]))
        scatter_pieces(i * chunk, total, outs)
    for copy in copies:
        copy.wait()


def expert_weights_kernel(xa, xb, ya, yb, ha, hb, da, db, *outs):
    chunk = 256
    model = xa.shape[1]
    first, second = outs if len(outs) == 2 else (outs[0].at[0:model], outs[0].at[model:])
    for i in range(model // chunk):
        at = slice(i * chunk, (i + 1) * chunk)
        first[at, :] = (dot(xa[:, at], da[...], TN) + dot(xb[:, at], db[...], TN)).astype(
            first.dtype
        )
    for i in range(ha.shape[1] // chunk):
        at = slice(i * chunk, (i + 1) * chunk)
        second[at, :] = (dot(ha[:, at], ya[...], TN) + dot(hb[:, at], yb[...], TN)).astype(
            second.dtype
        )


def expert_sums_kernel(xa, xb, ya, yb, ha, hb, da, db, far_first, far_second, first_ref, second_ref):
    first_ref[...] = dot(xa[...], da[...], TN) + dot(xb[...], db[...], TN) + far_first[...].astype(F32)
    second_ref[...] = (
        dot(ha[...], ya[...], TN) + dot(hb[...], yb[...], TN) + far_second[...].astype(F32)
    )


def expert_sums(xa, xb, ya, yb, ha, hb, da, db, far, chunk=128):
    rows, model = xa.shape
    ff = ha.shape[1]
    steps = model // chunk
    column = pl.BlockSpec((rows, chunk), lambda i: (0, i))
    whole = pl.BlockSpec((rows, ff), lambda i: (0, 0))
    out = pl.BlockSpec((chunk, ff), lambda i: (i, 0))
    return pl.pallas_call(
        expert_sums_kernel,
        out_shape=[jax.ShapeDtypeStruct((model, ff), F32), jax.ShapeDtypeStruct((ff, model), F32)],
        grid=(steps,),
        in_specs=[column, column, whole, whole, column, column, whole, whole]
        + [out, pl.BlockSpec((chunk, ff), lambda i: (i + steps, 0))],
        out_specs=[out, out],
        compiler_params=pltpu.CompilerParams(vmem_limit_bytes=14 * MIB),
        cost_estimate=pl.CostEstimate(flops=int(SUMS * 1.15e9), bytes_accessed=0, transcendentals=0),
        name="expert_sums_kernel",
    )(*(pltpu.with_memory_space_constraint(v, pltpu.HBM) for v in (xa, xb, ya, yb, ha, hb, da, db, far, far)))


def pick_rows(column, got_ref):
    lane = lax.broadcasted_iota(jnp.int32, (column.shape[0], got_ref.shape[0]), 1)
    return dot(jnp.where(lane == column, 1.0, 0.0).astype(BF16), got_ref[...])


def combine_kernel(pieces, *refs):
    (middle_ref, normed_ref, g_ref, router_ref, back_ref, embed_ref, embed_t,
     temper_ref, route_ref, col_ref,
     result_ref, grad_ref, stats_ref, got_ref) = refs[pieces:]
    gather_pieces(refs[:pieces], got_ref)
    count = normed_ref.shape[0]
    normed = normed_ref[...]
    embed = embed_ref[...]
    depth = embed.shape[1]
    temper = temper_ref[...]
    projected, length, unit, logits, probs, chosen, gating = route_forward(
        normed, router_ref[...], embed, temper, route_ref[...]
    )
    gate_col = jnp.broadcast_to(gating, (8, count)).T[:, 0:1]
    chunk = 128
    dots = []
    for i in range(count // chunk):
        at = slice(i * chunk, (i + 1) * chunk)
        token_out = pick_rows(col_ref[at, :], got_ref)
        result_ref[at, :] = (middle_ref[at, :] + gate_col[at, :] * token_out).astype(BF16)
        dots.append(jnp.sum(g_ref[at, :].astype(F32) * token_out, axis=1, keepdims=True))
    grad_gate = jnp.broadcast_to(jnp.concatenate(dots, axis=0), (count, 128)).T[0:1, :]
    dlogits = grad_gate * gating * (chosen - probs)
    draw = dlogits / temper
    anchor_t = embed_t[...] * lax.rsqrt(
        jnp.sum(embed_t[...] * embed_t[...], axis=0, keepdims=True) + 1e-06
    )
    dunit = dot(anchor_t, draw, precision=HIGHEST)
    danchor = dot(draw, unit, NT, precision=HIGHEST)
    size = lax.rsqrt(jnp.sum(embed * embed, axis=1, keepdims=True) + 1e-06)
    dembed = size * danchor - embed * (
        size * size * size * jnp.sum(embed * danchor, axis=1, keepdims=True)
    )
    dproj = length * dunit - projected * (
        length * length * length * jnp.sum(projected * dunit, axis=0, keepdims=True)
    )
    high, mid, low = (part.astype(F32) for part in split3(dproj))
    three = dot(jnp.concatenate([high, mid, low], axis=0).astype(BF16), normed)
    stats_ref[...] = jnp.zeros_like(stats_ref)
    stats_ref[0:depth, :] = three[0:depth] + three[depth : 2 * depth] + three[2 * depth :]
    stacked = jnp.concatenate(
        [high, high, high, mid, mid, low, jnp.zeros((2 * depth, count), F32)], axis=0
    )
    grad_ref[...] = dot(stacked.T.astype(BF16), back_ref[...])
    spent = -jnp.sum(jnp.sum(dlogits * logits / temper, axis=0, keepdims=True), axis=1, keepdims=True)
    counts = dot(jnp.ones((8, count), F32), chosen, NT)
    number = embed.shape[0]
    lane = lax.broadcasted_iota(jnp.int32, (8, 128), 1)
    row = lax.broadcasted_iota(jnp.int32, (8, 128), 0)
    counts = jnp.concatenate([counts, jnp.zeros((8, 128 - number), F32)], axis=1)
    stats_ref[depth : depth + 8, 0:128] = jnp.where(
        row == 1, counts, jnp.where((row == 2) & (lane == 0), spent, 0.0)
    )
    stats_ref[depth + 8 : depth + 8 + number, 0:depth] = dembed


def middle_back_kernel(pieces, *refs):
    got_ref = refs[-1]
    gather_pieces(refs[:pieces], got_ref)
    (route_grad, middle_ref, gain_ref, g_ref, col_ref, w0, far_ref,
     grad_out, low_ref, m0, m1, m2, m3, dgain_ref, grad_ref, sem) = refs[pieces:-1]
    count = middle_ref.shape[0]
    chunk = 128
    width = m0.shape[0]
    dgain = None
    for i in range(count // chunk):
        at = slice(i * chunk, (i + 1) * chunk)
        grad = pick_rows(col_ref[at, :], got_ref) + route_grad[at, :]
        unit, scale = normalize(middle_ref[at, :])
        part = jnp.sum(grad * unit, axis=0, keepdims=True)
        dgain = part if dgain is None else dgain + part
        total = g_ref[at, :].astype(F32) + normalize_back(unit, scale, grad * gain_ref[...])
        grad_ref[at, :] = total
        low = total.astype(BF16)
        low_ref[at, :] = low
        m0[:, at] = dot(w0[...], low, NT).astype(BF16)
        for k, ref in enumerate((m1, m2, m3)):
            weight = far_ref[k * width : (k + 1) * width, :]
            ref[:, at] = dot(weight, low, NT).astype(BF16)
    dgain_ref[...] = dgain
    copy = pltpu.make_async_copy(grad_ref, grad_out, sem)
    copy.start()
    copy.wait()


def two_terms(values):
    high = values.astype(BF16)
    return high, (values - high.astype(F32)).astype(BF16)


def mix_weights_kernel(*refs):
    (core_ref, mixed_ref, low_ref, stats_ref, dgain_ref, embed_ref,
     mine_out, other_ref, part_ref, small_ref, mine_ref, sem) = refs
    width = part_ref.shape[0]
    half = width // 2
    size = stats_ref.shape[0] // 2
    core = core_ref[0]
    near, away = pl.multiple_of(core * half, 16), pl.multiple_of((1 - core) * half, 16)
    for k in range(4):
        part_ref[...] = dot(mixed_ref[k * width : (k + 1) * width, :], low_ref[...])
        at = slice(k * half, (k + 1) * half)
        mine_ref[at, :] = part_ref[pl.ds(near, half), :]
        other_ref[at, :] = part_ref[pl.ds(away, half), :].astype(BF16)
    row = lax.broadcasted_iota(jnp.int32, stats_ref.shape, 0)
    small_ref[...] = stats_ref[...] + jnp.where(row == embed_ref.shape[1], dgain_ref[...], 0.0)
    near, away = pl.multiple_of(core * size, 16), pl.multiple_of((1 - core) * size, 16)
    mine_ref[4 * half :, :] = small_ref[pl.ds(near, size), :]
    high, low = two_terms(small_ref[pl.ds(away, size), :])
    other_ref[4 * half : 4 * half + size, :] = high
    other_ref[4 * half + size :, :] = low
    copy = pltpu.make_async_copy(mine_ref, mine_out, sem)
    copy.start()
    copy.wait()


def mix_head_kernel(half, mine_ref, got_ref, own_ref, o1, o2, o3):
    size = mine_ref.shape[0] - 4 * half
    small = (
        mine_ref[4 * half :, :]
        + got_ref[4 * half : 4 * half + size, :].astype(F32)
        + got_ref[4 * half + size :, :].astype(F32)
    )
    high, low = two_terms(small)
    own_ref[0:half, :] = mine_ref[0:half, :] + got_ref[0:half, :].astype(F32)
    own_ref[half:, :] = small
    for k, ref in enumerate((o1, o2, o3), 1):
        at = slice(k * half, (k + 1) * half)
        ref[0:half, :] = (mine_ref[at, :] + got_ref[at, :].astype(F32)).astype(BF16)
        ref[half : half + size, :] = high
        ref[half + size :, :] = low


def mix_share_kernel(half, place_ref, own_ref, a_ref, b_ref, c_ref, *refs):
    *sends, sum_ref = refs
    size = own_ref.shape[0] - half
    rows = own_ref[0:half, :]
    small = own_ref[half:, :]
    for ref in (a_ref, b_ref, c_ref):
        rows += ref[0:half, :].astype(F32)
        small += ref[half : half + size, :].astype(F32) + ref[half + size :, :].astype(F32)
    sum_ref[0:half, :] = rows
    sum_ref[half : half + size, :] = small
    rest = sum_ref.shape[0] - half - size
    if rest:
        sum_ref[half + size :, :] = jnp.zeros((rest, sum_ref.shape[1]), F32)
    cut_shares(place_ref, sum_ref, sends)


def cut_shares(place_ref, sum_ref, sends):
    share = sum_ref.shape[0] // len(sends)
    for k, ref in enumerate(sends):
        at = pl.ds(pl.multiple_of((place_ref[0] ^ k) * share, 8), share)
        ref[...] = sum_ref[at, :].astype(ref.dtype)


def wo_kernel(core_ref, a_ref, b_ref, c_ref, far_ref, out_ref):
    half = a_ref.shape[0]
    core = core_ref[0]
    for k, ref in enumerate((a_ref, b_ref, c_ref)):
        near = pl.multiple_of((2 * k + core) * half, 16)
        away = pl.multiple_of((2 * k + 1 - core) * half, 16)
        out_ref[pl.ds(near, half), :] = ref[...]
        out_ref[pl.ds(away, half), :] = far_ref[k * half : (k + 1) * half, :]


def proj_weights_kernel(
    core_ref, n0, n1, q0, k0, v0, q1, k1, v1, wq, wk, wv, gain_ref,
    mine_ref, other_ref, dgain_ref, sum_ref,
):
    width = wq.shape[0]
    total = None
    for j, (first, second, weight) in enumerate(((q0, q1, wq), (k0, k1, wk), (v0, v1, wv))):
        rows = dot(first[...], n0[...], TN) + dot(second[...], n1[...], TN)
        sum_ref[j * width : (j + 1) * width, :] = rows
        part = jnp.sum(rows * weight[...].astype(F32), axis=0, keepdims=True)
        total = part if total is None else total + part
    rest = sum_ref.shape[0] - 3 * width
    if rest:
        sum_ref[3 * width :, :] = jnp.zeros((rest, sum_ref.shape[1]), F32)
    dgain = total / gain_ref[...]
    dgain_ref[...] = jnp.broadcast_to(dgain, dgain_ref.shape)
    half = mine_ref.shape[0]
    other_ref[half:, :] = jnp.broadcast_to(dgain, (EXTRA, dgain.shape[1])).astype(BF16)
    core = core_ref[0]
    mine_ref[...] = sum_ref[pl.ds(pl.multiple_of(core * half, 16), half), :]
    other_ref[0:half, :] = sum_ref[pl.ds(pl.multiple_of((1 - core) * half, 16), half), :].astype(BF16)


def share_kernel(shares, packed, place_ref, mine_ref, got_ref, dgain_ref, *refs):
    mix, refs = refs[:shares], refs[shares:]
    own_ref, mix_ref, total_ref, *sends, sum_ref = refs
    share = own_ref.shape[0]
    half = mine_ref.shape[0]
    place = place_ref[0]
    sum_ref[...] = mine_ref[...] + got_ref[0:half, :].astype(F32)
    dgain = dgain_ref[...] + got_ref[half:, :][0:8, :].astype(F32)
    total_ref[...] = dgain
    dgain = jnp.broadcast_to(dgain[0:1, :], (EXTRA, dgain.shape[1])).astype(BF16)
    rest = mix[0][...]
    for ref in mix[1:]:
        rest += ref[...]
    high, low = two_terms(rest)
    if packed:
        size = high.shape[0] // 2
        last = jnp.full((size, high.shape[1]), place, jnp.int32) == shares - 1
        rows = jnp.where(last, low[0:size].astype(F32), high[size:].astype(F32))
        high = jnp.concatenate([high[0:size], rows.astype(BF16)], axis=0)
    mix_ref[...] = high
    own_ref[...] = sum_ref[pl.ds(pl.multiple_of(place * share, 16), share), :]
    for k, ref in enumerate(sends, 1):
        at = pl.ds(pl.multiple_of((place ^ k) * share, 16), share)
        ref[0:share, :] = sum_ref[at, :].astype(BF16)
        ref[share : share + EXTRA, :] = dgain
        ref[share + EXTRA :, :] = high


def sum_kernel(own_ref, dgain_ref, *refs):
    *came, out_ref, total_ref = refs
    rows, dgain = own_ref[...], dgain_ref[...]
    share = rows.shape[0]
    for ref in came:
        rows += ref[0:share, :].astype(F32)
        dgain += ref[share : share + EXTRA, :][0:8, :].astype(F32)
    out_ref[...] = rows.astype(BF16)
    total_ref[...] = dgain


def place_kernel(shares, share, place_ref, *refs):
    second, mix_ref, first = refs[:shares], refs[shares], refs[shares + 1 : 2 * shares]
    out_ref = refs[2 * shares]
    size = mix_ref.shape[0]
    place = place_ref[0]
    start = share * shares
    for k in range(shares):
        there = place ^ k
        rest = mix_ref[...] if k == 0 else first[k - 1][share + EXTRA :, :]
        out_ref[pl.ds(pl.multiple_of(there * share, 16), share), :] = second[k][...]
        out_ref[pl.ds(pl.multiple_of(start + there * size, 16), size), :] = rest


def join_kernel(half, mix, packed, core_ref, near_ref, far_ref, dgain_ref, dgain_y, *refs):
    (q_ref, k_ref, v_ref, o_ref, router_ref, small_ref, embed_ref, gain_ref,
     sum_ref, rest_ref) = refs
    core = core_ref[0]
    width = o_ref.shape[0] // 2
    size = rest_ref.shape[0] // 2
    for ref, side in ((near_ref, core), (far_ref, 1 - core)):
        sum_ref[pl.ds(pl.multiple_of(side * half, 16), half), :] = ref[0:half, :].astype(F32)
        rows = ref[half : half + mix, :].astype(F32)
        o_ref[pl.ds(pl.multiple_of(side * width, 16), width), :] = rows[0:width]
        rest = rows[width : width + size]
        if packed:
            rest += rows[width + size : width + 2 * size]
        rest_ref[pl.ds(pl.multiple_of(side * size, 16), size), :] = rest
    start = 0
    for out in (q_ref, k_ref, v_ref):
        out[...] = sum_ref[start : start + out.shape[0], :]
        start += out.shape[0]
    depth = router_ref.shape[0]
    router_ref[...] = rest_ref[0:depth, :]
    small_ref[...] = rest_ref[depth : depth + 8, :]
    embed_ref[...] = rest_ref[depth + 8 : depth + 8 + embed_ref.shape[0], 0:depth]
    gain_ref[...] = dgain_ref[...] + dgain_y[...]


def final_kernel(x_ref, gain_ref, grad_ref, last_a, last_b, *refs):
    *sides, out_ref = refs
    chunk = last_b.shape[0] // (len(sides) // 3)
    for s in range(len(sides) // 3):
        own, from_x, from_y = sides[3 * s : 3 * s + 3]
        for part, (first, last) in enumerate(((from_x, last_a), (from_y, last_b))):
            inner = slice(part * chunk, (part + 1) * chunk)
            at = slice((2 * s + part) * chunk, (2 * s + part + 1) * chunk)
            grad = own[inner, :] + first[0:chunk, :].astype(F32)
            grad += last[s * chunk : (s + 1) * chunk, :].astype(F32)
            unit, scale = normalize(x_ref[at, :].astype(F32))
            out_ref[at, :] = grad_ref[at, :] + normalize_back(unit, scale, grad * gain_ref[...])


def relay_kernel(*refs):
    *sides, out_a, out_b = refs
    count = len(sides) // 4
    chunk = out_b.shape[0] // count
    for s in range(count):
        keep_a, keep_b, from_x, from_y = sides[4 * s : 4 * s + 4]
        at = slice(s * chunk, (s + 1) * chunk)
        out_a[at, :] = (keep_a[...] + from_x[chunk:, :].astype(F32)).astype(BF16)
        out_b[at, :] = (keep_b[...] + from_y[chunk:, :].astype(F32)).astype(BF16)


def swap_head(values, bit):
    size = lax.axis_size("head")
    return lax.ppermute(values, "head", [(i, i ^ bit) for i in range(size)])


def swap_expert(values, bit):
    size = lax.axis_size("expert")
    return lax.ppermute(values, "expert", [(i, i ^ bit) for i in range(size)])


def swap_pair(values, even, odd):
    heads, experts = lax.axis_size("head"), lax.axis_size("expert")
    moves = [
        (h * experts + e, (h ^ (odd if e % 2 else even)) * experts + e)
        for h in range(heads)
        for e in range(experts)
    ]
    return lax.ppermute(values, ("head", "expert"), moves)


def swap_pieces(pieces):
    return [pieces[0]] + [swap_expert(piece, 2 * k) for k, piece in enumerate(pieces) if k]


def local(
    block_entries,
    passage_labels,
    assigned_specialist,
    buffer_places,
    mixing_scaling_factor,
    asker_projection,
    address_projection,
    content_projection,
    final_mixing_projection,
    specialist_scaling_factor,
    dispatcher_projection,
    specialist_anchors_vector,
    softening_coefficient,
    specialist_widen_factors,
    specialist_shrink_factors,
    incoming_gradient,
):
    seqs, span, model = block_entries.shape
    length = passage_labels.shape[1]
    blocks = length // span
    rows = seqs * span
    width = asker_projection.shape[1]
    heads = width // HSZ
    experts, depth = specialist_anchors_vector.shape
    capacity = rows // experts
    experts_axis = lax.axis_size("expert")
    head_index = lax.axis_index("head")
    expert_index = lax.axis_index("expert")
    half = span // 2

    x_flat = block_entries.reshape(rows, model)
    g_flat = incoming_gradient.reshape(rows, model)
    gain_attn = mixing_scaling_factor.reshape(1, model)
    gain_moe = specialist_scaling_factor.reshape(1, model)
    widen = specialist_widen_factors.reshape(model, -1)
    shrink = specialist_shrink_factors.reshape(-1, model)
    ff = widen.shape[1]
    wq, wk, wv = asker_projection.T, address_projection.T, content_projection.T
    core = (expert_index % 2).astype(jnp.int32).reshape(1)
    place = (expert_index // 2).astype(jnp.int32).reshape(1)

    order = Order()
    shares = experts_axis // 2
    quarter = width // 2
    piece = rows // shares
    mid = shares // 2
    stats_rows = -(-(depth + 8 + experts) // 32) * 32
    size = stats_rows // 2

    top, bottom = call(
        functools.partial(norm_kernel, 0), [((half, model), BF16)] * 2, (x_flat, gain_attn)
    )
    x_top, y_bottom = swap_head(top, 1), swap_head(bottom, 2)
    order.mark(top)
    later = call(
        functools.partial(norm_kernel, 1), [((span, model), BF16)], order((x_flat, gain_attn))
    )
    order.mark(*later)
    x_bottom, y_top = swap_head(order(bottom), 1), swap_head(order(top), 2)
    relay_y, relay_x = swap_head(x_top, 2), swap_head(y_bottom, 1)
    order.mark(x_top, y_bottom, x_bottom, y_top)
    order.arrived(relay_y)
    later = order(later)
    parts = [(top, bottom, x_top, x_bottom, y_top, y_bottom, relay_y, relay_x)] + [
        (n,) + tuple(swap_head(n, k) for k in (1, 2, 3)) for n in later
    ]

    *labels, route_row, col_row, col_col = call(
        functools.partial(prep_kernel, experts),
        [((1, length), jnp.int32)] * seqs + [((1, rows), jnp.int32)] * 2 + [((rows, 1), jnp.int32)],
        (
            head_index.astype(jnp.int32).reshape(1), expert_index.astype(jnp.int32).reshape(1),
            *order((passage_labels, assigned_specialist, buffer_places)),
        ),
        smem=2,
        micros=BESIDE,
    )
    high, med, low = split3(dispatcher_projection.T)
    router_split = jnp.concatenate([high, med, low], axis=0)
    router_back = jnp.concatenate(
        [high, med, low, high, med, high, jnp.zeros((2 * depth, model), BF16)], axis=0
    )
    temper = softening_coefficient.reshape(1, 1)

    def attend(s, blocks, earlier):
        return call(
            functools.partial(attend_kernel, len(earlier)),
            [((length, width), BF16, pltpu.HBM)] * 3
            + [((length, model), BF16, pltpu.HBM), ((width, length), F32, pltpu.HBM)]
            + [((width, (s + 1) * span), BF16)] * 4
            + [((heads, length), F32)],
            (
                *blocks, *earlier, wq, wk, wv, labels[s],
            ),
            scratch=[pltpu.VMEM((length, width), BF16)] * 3
            + [
                pltpu.VMEM((heads, length, width), BF16),
                pltpu.VMEM((width, length), BF16),
                pltpu.VMEM((width, length), F32),
                pltpu.VMEM((length, 1), F32),
                pltpu.SemaphoreType.DMA((12,)),
            ],
            micros=ATTEND,
        )

    order.mark(
        relay_x, relay_y, *labels, router_split, router_back
    )
    attended = [attend(0, order(parts[0]), ())]
    order.mark(attended[0][5])
    half_mix = lax.dynamic_slice_in_dim(
        final_mixing_projection, (expert_index % 2) * quarter, quarter, 0
    )
    half_mix = order(half_mix)
    wo_parts = [swap_head(half_mix, k) for k in (1, 2, 3)]
    attended.append(attend(1, order(parts[1]), attended[0][5:9]))
    order.mark(attended[1][5])
    mixed = [attended[1][5]] + [swap_head(attended[1][5 + k], k) for k in (1, 2, 3)]
    wo_parts = order(wo_parts)
    (wo_far,) = call(
        wo_kernel,
        [((3 * width, model), BF16)],
        (core, *wo_parts, swap_expert(jnp.concatenate(wo_parts, axis=0), 1)),
        smem=1,
    )
    wo = (final_mixing_projection, wo_far)
    order.mark(wo_far)
    mixed = order(mixed)
    order.mark(*mixed)
    far = swap_pair(order(jnp.concatenate([widen, shrink], axis=0)), 1, 2)

    middle, normed_moe, mixed_stash, wo_stash, gr_a, gr_b, tok_a, tok_b = call(
        middle_kernel,
        [
            ((rows, model), F32, pltpu.HBM),
            ((rows, model), BF16, pltpu.HBM),
            ((4 * width, rows), BF16, pltpu.HBM),
            ((3 * width, model), BF16, pltpu.HBM),
        ]
        + [((rows // 2, model), BF16, pltpu.HBM)] * 2
        + [((rows // 2, model), BF16)] * 2,
        (
            *mixed, *wo, x_flat, gain_moe, router_split, specialist_anchors_vector, temper,
            route_row, col_row, g_flat,
        ),
        scratch=[
            pltpu.VMEM((rows, model), F32),
            pltpu.VMEM((rows, model), BF16),
            pltpu.VMEM((rows // 2, model), BF16),
            pltpu.VMEM((rows // 2, model), BF16),
            pltpu.SemaphoreType.DMA((9,)),
        ],
    )

    def join_cores(first, near):
        if capacity % 16 == 0:
            return call(cores_kernel, [((piece, model), BF16)] * shares, (first, near))
        return [
            jnp.concatenate(
                [first[k * capacity : (k + 1) * capacity], near[k * capacity : (k + 1) * capacity]],
                axis=0,
            )
            for k in range(shares)
        ]

    def half_of(pieces, micros=0.02):
        return call(half_kernel, [((rows // 2, model), BF16)], tuple(pieces), micros=micros)[0]

    def pair(values):
        return swap_pair(values, 2, 1)

    def add(own, values):
        return [
            (part + values[k * piece : (k + 1) * piece].astype(F32)).astype(BF16)
            for k, part in enumerate(own)
        ]

    def second_half(pieces, rest=(), micros=0.02):
        count = len(pieces)
        if capacity % 16 == 0:
            size = count * capacity + sum(part.shape[0] for part in rest)
            return call(
                functools.partial(second_kernel, count),
                [((size, model), BF16)],
                (*pieces, *rest),
                micros=micros,
            )[0]
        return jnp.concatenate([part[capacity:] for part in pieces] + list(rest), axis=0)

    def expert_outs(dtype):
        if dtype == F32:
            return [((piece, model), F32)] * shares
        return [((rows // 2, model), dtype)] * 2

    def expert(two, dtype, micros):
        return call(
            functools.partial(expert_kernel, 2),
            [((rows, model), BF16, pltpu.HBM), ((rows, ff), BF16, pltpu.HBM)]
            + [((rows, model), BF16), ((rows, ff), BF16)]
            + [((rows, ff), F32)] * 2
            + expert_outs(dtype),
            (*two, widen, shrink, far),
            scratch=[pltpu.VMEM((rows, ff), BF16), pltpu.SemaphoreType.DMA((3,))],
            micros=micros,
        )

    def expert_back(two, slopes, dtype, micros):
        return call(
            functools.partial(expert_back_kernel, 2),
            [((rows, model), BF16, pltpu.HBM), ((rows, ff), BF16, pltpu.HBM)]
            + [((rows, model), BF16), ((rows, ff), BF16)]
            + expert_outs(dtype),
            (*two, widen, shrink, far, *slopes),
            scratch=[pltpu.VMEM((rows, ff), BF16), pltpu.SemaphoreType.DMA((3,))],
            micros=micros,
        )

    cut = shares // 2
    x_pieces = swap_pieces(join_cores(tok_a, swap_expert(tok_b, 1)))
    y_sends = join_cores(gr_a, swap_expert(gr_b, 1))
    order.mark(y_sends[0], *x_pieces[1:cut])
    x_half = half_of(order(x_pieces[:cut]))
    x_far_half = pair(x_half)
    order.mark(x_half, *x_pieces[cut:], far)
    x_rest = half_of(order(x_pieces[cut:]), 2 * BESIDE)
    x_far_rest = pair(x_rest)
    order.mark(x_rest)
    y_pieces = swap_pieces(order(y_sends))
    x_far_half = order(x_far_half)
    order.arrived(x_far_half)
    x_own_kept, h0_own, x_own, h1_own, p0_own, p1_own, *out_own = expert(order((x_half, x_rest)), F32, BESIDE)
    order.mark(h1_own)
    x_far_kept, h0_far, x_far, h1_far, p0_far, p1_far, *out_far = expert(
        (x_far_half, order(x_far_rest)), BF16, 0.02
    )
    order.mark(h1_far)
    out_far = [pair(part) for part in out_far]
    y_pieces = order(y_pieces)
    y_half = half_of(y_pieces[:cut])
    y_rest = half_of(y_pieces[cut:], BESIDE)
    order.mark(y_half, y_rest)
    out_rest = add(out_own[cut:], order(out_far[1]))
    order.mark(*out_rest)
    ret_rest = [swap_expert(part, 2 * k) for k, part in enumerate(out_rest, cut)]
    y_far_half, y_far_rest = pair(order(y_half)), pair(order(y_rest))
    y_own_kept, d0_own, y_own, d1_own, *dx_own = expert_back(
        order((y_half, y_rest)), (p0_own, p1_own), F32, BESIDE
    )
    order.mark(d1_own)
    out_half = add(out_own[:cut], order(out_far[0]))
    order.mark(*out_half)
    ret_half = swap_pieces(out_half)
    y_far_kept, d0_far, y_far, d1_far, *dx_far = expert_back(
        order((y_far_half, y_far_rest)), (p0_far, p1_far), BF16, 0.02
    )
    order.mark(d1_far)
    dx_far = [pair(part) for part in dx_far]
    ret_rest = order(ret_rest)
    ret_second = second_half(ret_rest, (), BESIDE)
    order.mark(ret_second)
    ret_half = order(ret_half)
    ret_second = second_half(ret_half, (ret_second,), BESIDE)
    ret_pieces = ret_half + ret_rest
    order.mark(ret_second)

    def expert_weights(h_own, h_far, d_own, d_far, outs, micros):
        return call(
            expert_weights_kernel,
            outs,
            (x_own, x_far, y_own, y_far, h_own, h_far, d_own, d_far),
            micros=micros,
        )

    (dw_far,) = expert_weights(
        h1_own, h1_far, d1_own, order(d1_far), [((model + ff, model), BF16)], 0.02
    )
    order.mark(dw_far)
    dx_rest = add(dx_own[cut:], order(dx_far[1]))
    order.mark(*dx_rest)
    back_rest = [swap_expert(part, 2 * k) for k, part in enumerate(dx_rest, cut)]
    dx_half = add(dx_own[:cut], order(dx_far[0]))
    order.mark(*dx_half)
    back_half = swap_pieces(dx_half)
    dw_far = swap_pair(order(dw_far), 1, 2)
    ret_second = swap_expert(ret_second, 1)
    result, route_grad, stats = call(
        functools.partial(combine_kernel, shares + 1),
        [((rows, model), BF16), ((rows, model), F32), ((stats_rows, model), F32)],
        (
            *ret_pieces, order(ret_second), middle, normed_moe, g_flat, router_split, router_back,
            specialist_anchors_vector, specialist_anchors_vector.T, temper, route_row, col_col,
        ),
        scratch=[pltpu.VMEM((rows + rows // 2, model), BF16)],
    )
    order.mark(route_grad)
    back_rest = order(back_rest)
    back_second = second_half(back_rest, (), BESIDE)
    order.mark(back_second)
    back_half = order(back_half)
    back_second = swap_expert(second_half(back_half, (back_second,), BESIDE), 1)
    back_pieces = back_half + back_rest
    grad_middle, grad_low, *grad_mixed, dgain_moe = call(
        functools.partial(middle_back_kernel, shares + 1),
        [((rows, model), F32, pltpu.HBM), ((rows, model), BF16)]
        + [((width, rows), BF16)] * 4
        + [((1, model), F32)],
        (
            *back_pieces, back_second, route_grad, middle, gain_moe, g_flat, col_col,
            final_mixing_projection, wo_stash,
        ),
        scratch=[
            pltpu.VMEM((rows, model), F32),
            pltpu.SemaphoreType.DMA,
            pltpu.VMEM((rows + rows // 2, model), BF16),
        ],
    micros=6.0,
    )
    grads = [grad_mixed[0]] + [swap_head(grad_mixed[k], k) for k in (1, 2, 3)]

    mix_mine, mix_other = call(
        mix_weights_kernel,
        [((4 * quarter + size, model), F32, pltpu.HBM), ((4 * quarter + 2 * size, model), BF16)],
        (core, mixed_stash, grad_low, stats, dgain_moe, specialist_anchors_vector),
        scratch=[
            pltpu.VMEM((width, model), F32),
            pltpu.VMEM((stats_rows, model), F32),
            pltpu.VMEM((4 * quarter + size, model), F32),
            pltpu.SemaphoreType.DMA,
        ],
        smem=1,
        micros=2.0,
    )
    order.mark(mix_other)
    mix_mine = order(mix_mine)
    mix_own, *mix_sends = call(
        functools.partial(mix_head_kernel, quarter),
        [((quarter + size, model), F32)] + [((quarter + 2 * size, model), BF16)] * 3,
        (mix_mine, swap_expert(mix_other, 1)),
    )
    order.mark(mix_own)
    grads = order(grads)
    dw_far = order(dw_far)
    order.mark(*grads, dw_far)
    mix_got = [swap_head(order(part), k) for k, part in enumerate(mix_sends, 1)]

    def attend_back(s, blocks):
        q, k, v, _, out = attended[s][:5]
        return call(
            functools.partial(attend_back_kernel, s),
            [((length, width), BF16)] * 3
            + [((span, model), F32)]
            + [((half, model), F32)] * 2
            + [((span, model), BF16)] * 2,
            (
                q, k, v, out, *blocks, attended[s][9],
                labels[s], wq, wk, wv,
            ),
            scratch=[
                pltpu.VMEM((heads, length, width), BF16),
                pltpu.VMEM((heads, length, width), BF16),
                pltpu.VMEM((width, length), BF16),
                pltpu.VMEM((width, length), BF16),
                pltpu.VMEM((length, width), F32),
                pltpu.VMEM((length, width), F32),
                pltpu.VMEM((length, 1), F32),
                pltpu.VMEM((length, heads * span), BF16),
                pltpu.VMEM((length, heads * span), BF16),
                pltpu.VMEM((width, model), BF16),
                pltpu.VMEM((width, model), BF16),
                pltpu.VMEM((width, model), BF16),
                pltpu.SemaphoreType.DMA((3,)),
            ],
            kept=3,
            micros=ATTEND_BACK if s else BACK_FIRST,
        )

    back0 = attend_back(0, grads)
    order.mark(back0[6])
    mix_got = order(mix_got)
    order.arrived(*mix_got)
    arrived0 = [swap_head(order(back0[6]), 1), swap_head(order(back0[7]), 2)]
    mix_rows = -(-(quarter + size) // (16 * shares)) * 16 * shares
    mix_share, *mix_sends = call(
        functools.partial(mix_share_kernel, quarter),
        [((mix_rows // shares, model), F32)] * shares,
        (place, mix_own, *mix_got),
        scratch=[pltpu.VMEM((mix_rows, model), F32)],
        smem=1,
    )
    order.mark(mix_share)
    mix_came = [swap_expert(part, 2 * k) for k, part in enumerate(mix_sends, 1)]
    back1 = attend_back(1, order(grads))
    order.mark(back1[6])
    mix_came = order(mix_came)
    order.arrived(*mix_came)
    arrived0 = order(arrived0)
    order.arrived(*arrived0)
    unit = 32 * shares
    proj_rows = -(-3 * width // unit) * unit
    proj_half = proj_rows // 2
    share = proj_half // shares
    mix_part = mix_rows // shares
    packed = mix_part == 2 * size and quarter % mix_part == 0
    arrived1 = [swap_head(order(back1[6]), 1), swap_head(order(back1[7]), 2)]
    proj_mine, proj_other, dgain = call(
        proj_weights_kernel,
        [((proj_half, model), F32), ((proj_half + EXTRA, model), BF16), ((8, model), F32)],
        (
            core, attended[0][3], attended[1][3], *back0[:3], *order(back1[:3]),
            wq, wk, wv, gain_attn,
        ),
        scratch=[pltpu.VMEM((proj_rows, model), F32)],
        smem=1,
    )
    order.mark(dgain)
    proj_own, mix_own, dgain, *sends = call(
        functools.partial(share_kernel, shares, packed),
        [((share, model), F32), ((mix_part, model), BF16), ((8, model), F32)]
        + [((share + EXTRA + mix_part, model), BF16)] * (shares - 1),
        (place, proj_mine, swap_expert(proj_other, 1), dgain, mix_share, *mix_came),
        scratch=[pltpu.VMEM((proj_half, model), F32)],
        smem=1,
    )
    order.mark(proj_own)
    first = [swap_expert(part, 2 * k) for k, part in enumerate(sends, 1)]
    grad_first, grad_second = expert_sums(
        x_own_kept, x_far_kept, y_own_kept, y_far_kept, h0_own, h0_far, d0_own, d0_far,
        order(dw_far),
    )
    order.mark(grad_first)
    arrived1 = order(arrived1)
    last_a, last_b = call(
        relay_kernel,
        [((seqs * half, model), BF16)] * 2,
        (*back0[4:6], *arrived0, *back1[4:6], *arrived1),
    )
    order.mark(last_a)
    last_a, last_b = swap_head(last_a, 2), swap_head(last_b, 1)
    first = order(first)
    message, dgain = call(
        sum_kernel,
        [((share, model), BF16), ((8, model), F32)],
        (proj_own, dgain, *first),
        micros=3 * BESIDE,
    )
    order.mark(message)
    second = [message] + [swap_expert(message, 2 * k) for k in range(1, shares)]
    last_a, last_b = order((last_a, last_b))
    order.arrived(last_a, last_b)
    dgain_x = swap_head(order(dgain), 1)
    (grad_tokens,) = call(
        final_kernel,
        [((rows, model), F32)],
        (
            x_flat, gain_attn, grad_middle, last_a, last_b,
            back0[3], *arrived0, back1[3], *arrived1,
        ),
        micros=FINAL,
    )
    order.mark(grad_tokens)
    dgain = dgain + order(dgain_x)
    order.mark(dgain)
    dgain_y = swap_head(dgain, 2)
    second = order(second)
    (whole,) = call(
        functools.partial(place_kernel, shares, share),
        [((proj_half + mix_rows, model), BF16)],
        (place, *second, mix_own, *first),
        smem=1,
    )
    dwq, dwk, dwv, grad_wo, drouter, small, dembed, dgain = call(
        functools.partial(join_kernel, proj_half, mix_rows, packed),
        [((width, model), F32)] * 4
        + [((depth, model), F32), ((8, model), F32), ((experts, depth), F32), ((8, model), F32)],
        (core, whole, swap_expert(whole, 1), dgain, dgain_y),
        scratch=[pltpu.VMEM((proj_rows, model), F32), pltpu.VMEM((stats_rows, model), F32)],
        smem=1,
    )
    load_share = small[1, 0:experts] * experts / (rows * lax.axis_size("head") * experts_axis)
    return (
        result.reshape(block_entries.shape),
        grad_tokens.reshape(block_entries.shape),
        dgain[0],
        dwq.T,
        dwk.T,
        dwv.T,
        grad_wo,
        small[0],
        drouter.T,
        dembed,
        small[2, 0:1],
        grad_first.reshape(specialist_widen_factors.shape),
        grad_second.reshape(specialist_shrink_factors.shape),
        load_share,
    )


def solution(mesh):
    in_specs = (
        P("expert", "head", None),
        P("expert", None),
        P("expert", "head"),
        P("expert", "head"),
        P(),
        P(None, "head"),
        P(None, "head"),
        P(None, "head"),
        P("head", None),
        P(),
        P(),
        P(),
        P(),
        P("expert", None, "head"),
        P("expert", "head", None),
        P("expert", "head", None),
    )
    out_specs = (
        P("expert", "head", None),
        P("expert", "head", None),
        P(),
        P(None, "head"),
        P(None, "head"),
        P(None, "head"),
        P("head", None),
        P(),
        P(),
        P(),
        P(),
        P("expert", None, "head"),
        P("expert", "head", None),
        P(),
    )
    return jax.shard_map(local, mesh=mesh, in_specs=in_specs, out_specs=out_specs, check_vma=False)
```
